256 devices in a mesh: dp: 4 (over x), ctx: 64 (over z, y, core).
Axes of the slice: x: 4, y: 4, z: 8, core: 2. Of those that a mesh axis runs over, the one named last changes fastest.
Arguments:
- inputs: bfloat16 [4, 16384, 4096], P('dp', 'ctx'), may hold values from -6 to 6
- query_weight: bfloat16 [4096, 128], P('dp'), may hold values from -0.09375 to 0.09375
- key_weight: bfloat16 [4096, 128], P('dp'), may hold values from -0.09375 to 0.09375
- value_weight: bfloat16 [4096, 2048], P('dp'), may hold values from -0.09375 to 0.09375
- lambda_weight: bfloat16 [4096, 320], P('dp'), may hold values from -0.09375 to 0.09375
- log_decay: float32 [4, 16384, 16], P('dp', 'ctx'), may hold values from -1 to 0, as said below
- norm_gain: float32 [2048], replicated, may hold values from 0.5 to 1.5
Outputs:
- outputs: bfloat16 [4, 16384, 2048], P('dp', 'ctx')
The draws below stay inside these ranges and needn't reach their ends.
Inputs may be any that keep to these rules, and one draw needn't show every extreme that they name: `log_decay`: entries are not positive.
All inputs are finite; a program needn't handle non-finite values.
Results may differ from the reference program's by a relative error of at most 0.0072.
Values may be sent and summed in bfloat16 or wider, within the bound.
No kernel may reach another device: no remote copies, remote signals or barrier semaphores. Data moves between devices by JAX's collectives and lax.ppermute only.
A program may use at most 128 MiB of HBM per device.

```python
import math
import jax
import jax.numpy as jnp
from jax import lax

D = 4096
HEADS = 16
HEAD = 128
STATE = 128
LAMBDAS = 20
TOK_DEV = 256
SEQUENCE_TOTAL = 4
SEQUENCE_SPAN = 16384
N_CTX = 64


def draw_log_decay(key, part):
    key_kind = jax.random.fold_in(key, 11)
    key_slow = jax.random.fold_in(key, 12)
    key_pick = jax.random.fold_in(key, 13)
    key_token = jax.random.fold_in(key, 14)
    key_block = jax.random.fold_in(key, 15)
    key_spurt = jax.random.fold_in(key, 16)
    key_keep = jax.random.fold_in(key, 17)
    key_width = jax.random.fold_in(key, 18)
    key_offset = jax.random.fold_in(key, 19)
    key_mass = jax.random.fold_in(key, 20)
    block_count = SEQUENCE_SPAN // TOK_DEV
    mixed_count = max(HEADS // 2, 1)
    fast_share = 0.5
    order = jax.random.permutation(key_kind, HEADS)
    mixed_head = order < mixed_count
    slow_rate = jnp.exp(jax.random.uniform(key_slow, (HEADS,), jnp.float32, math.log(0.05), math.log(0.4))) / SEQUENCE_SPAN
    block_shape = (SEQUENCE_TOTAL, block_count, 1, HEADS)
    fast_block = jnp.logical_and(jax.random.uniform(key_pick, block_shape, jnp.float32) < fast_share, mixed_head[None, None, None, :])
    token = jax.random.uniform(key_token, (SEQUENCE_TOTAL, block_count, TOK_DEV, HEADS), jnp.float32, 0.5, 2.0)
    blocks = jnp.exp(jax.random.uniform(key_block, block_shape, jnp.float32, -0.7, 0.7))
    slow_part = token * blocks * slow_rate[None, None, None, :]
    width = jax.random.randint(key_width, block_shape, max(TOK_DEV // 8, 1), TOK_DEV + 1)
    offset = jax.random.randint(key_offset, block_shape, 0, TOK_DEV) % (TOK_DEV - width + 1)
    position_in = jnp.arange(TOK_DEV, dtype=jnp.int32)[None, None, :, None]
    inside = jnp.logical_and(position_in >= offset, position_in < offset + width)
    mass = jnp.exp(jax.random.uniform(key_mass, block_shape, jnp.float32, math.log(8.0), math.log(16.0)))
    fast_part = jnp.where(inside, jnp.minimum(mass / width.astype(jnp.float32) * token, 1.0), slow_part)
    elementwise_rate = jnp.where(fast_block, fast_part, slow_part).reshape(SEQUENCE_TOTAL, SEQUENCE_SPAN, HEADS)
    spurt_index = jax.random.randint(key_spurt, (SEQUENCE_TOTAL, 3), 0, SEQUENCE_SPAN)
    token_place = jnp.arange(SEQUENCE_SPAN, dtype=jnp.int32)
    spurt_mask = jnp.any(token_place[None, :, None] == spurt_index[:, None, :], axis=-1)
    kept_entries = jax.random.uniform(key_keep, (SEQUENCE_TOTAL, SEQUENCE_SPAN, 1), jnp.float32, 0.55, 0.8)
    spurt_portion = jnp.where(spurt_mask[:, :, None], jnp.log(kept_entries), 0.0)
    return jnp.maximum(spurt_portion - elementwise_rate, -1.0).astype(jnp.float32)


def level_of(stream_key, extent, cuts, low, high):
    factor_of = 1.0
    for axis_at, shards_of in cuts:
        steps = jax.random.uniform(jax.random.fold_in(jax.random.fold_in(stream_key, 6), axis_at), (shards_of,), jnp.float32, low / len(cuts), high / len(cuts))
        factor_of = factor_of * jnp.repeat(jnp.exp(steps), extent[axis_at] // shards_of).reshape((-1,) + (1,) * (len(extent) - 1 - axis_at))
    return factor_of


def scatter_about(stream_key, shape, deviation, most, shards=(), held_as=jnp.bfloat16):
    drawn = jax.random.normal(stream_key, shape, jnp.float32) * deviation
    if len(shards) > 0:
        drawn = level_of(stream_key, shape, shards, -0.22, 0.18) * drawn
    return jnp.clip(drawn, min=-most, max=most).astype(held_as)


def setup_inputs(seed: int = 0) -> dict:
    keys = jax.random.split(jax.random.key(seed), 8)
    return {
        "inputs": scatter_about(keys[0], (SEQUENCE_TOTAL, SEQUENCE_SPAN, D), 1.0, 6.0, ((0, 4), (1, 64))),
        "query_weight": scatter_about(keys[1], (D, STATE), D ** -0.5, 0.09375, ((0, 4),)),
        "key_weight": scatter_about(keys[2], (D, STATE), D ** -0.5, 0.09375, ((0, 4),)),
        "value_weight": scatter_about(keys[3], (D, HEADS * HEAD), D ** -0.5, 0.09375, ((0, 4),)),
        "lambda_weight": scatter_about(keys[4], (D, HEADS * LAMBDAS), D ** -0.5, 0.09375, ((0, 4),)),
        "log_decay": draw_log_decay(jax.random.fold_in(keys[7], 71), 0),
        "norm_gain": jnp.clip(1.0 + 0.1 * jax.random.normal(keys[6], (HEADS * HEAD,), jnp.float32), 0.5, 1.5),
    }


HIGHEST = lax.Precision.HIGHEST

def level_masks(length):
    depth = length.bit_length() - 1
    token_place = jnp.arange(length, dtype=jnp.int32)
    differ = jnp.bitwise_xor(token_place[:, None], token_place[None, :])
    level = jnp.zeros((length, length), jnp.int32)
    for power in range(depth):
        level = level + (differ >= 1 << power).astype(jnp.int32)
    levels = jnp.arange(depth + 1, dtype=jnp.int32)
    return (level[None, :, :] == levels[:, None, None]).astype(jnp.float32)

def block_terms(query_rows, key_rows, value_rows, lambdas, log_decay, masks):
    length, heads = log_decay.shape
    state_dim = query_rows.shape[1]
    head_dim = value_rows.shape[1] // heads
    inner = masks.shape[0]
    weights_all = lambdas.reshape(length, heads, -1)
    cumulative = jnp.cumsum(log_decay, axis=0)
    scores = jnp.dot(query_rows, key_rows.T, preferred_element_type=jnp.float32) / math.sqrt(state_dim)
    level_weight = jnp.einsum('lts,thl->hts', masks, weights_all[:, :, :inner], precision=HIGHEST)
    token_place = jnp.arange(length, dtype=jnp.int32)
    causal = token_place[:, None] >= token_place[None, :]
    spread = jnp.transpose(cumulative)
    distance = spread[:, :, None] - spread[:, None, :]
    decay = jnp.exp(jnp.where(causal[None], distance, -jnp.inf))
    mix = (level_weight * decay * scores[None]).astype(jnp.bfloat16)
    values = value_rows.reshape(length, heads, head_dim)
    near = jnp.einsum('hts,shd->thd', mix.astype(jnp.float32), values.astype(jnp.float32), precision=HIGHEST)
    remain = jnp.exp(cumulative[-1][None, :] - cumulative)
    keyed = (key_rows.astype(jnp.float32)[:, None, :] * remain[:, :, None]).astype(jnp.bfloat16)
    state = jnp.einsum('chs,chd->hsd', keyed.astype(jnp.float32), values.astype(jnp.float32), precision=HIGHEST)
    total = jnp.exp(cumulative[-1])
    return (near, state, total, cumulative, weights_all)

def finish(mixed, norm_gain):
    heads = mixed.shape[-2]
    mean_square = lax.optimization_barrier(jnp.mean(mixed * mixed, axis=-1, keepdims=True))
    return (mixed * lax.rsqrt(mean_square + 1e-05) * norm_gain.reshape(heads, -1)).astype(jnp.bfloat16)

def reference(inputs, query_weight, key_weight, value_weight, lambda_weight, log_decay, norm_gain):
    bits = N_CTX.bit_length() - 1
    masks = level_masks(TOK_DEV)
    inner = masks.shape[0]
    scale = 1.0 / math.sqrt(STATE)

    def one_sequence(pair):
        sequence, decays = pair
        query_rows = jnp.dot(sequence, query_weight, preferred_element_type=jnp.float32).astype(jnp.bfloat16)
        key_rows = jnp.dot(sequence, key_weight, preferred_element_type=jnp.float32).astype(jnp.bfloat16)
        value_rows = jnp.dot(sequence, value_weight, preferred_element_type=jnp.float32).astype(jnp.bfloat16)
        lambdas = jax.nn.softplus(jnp.dot(sequence, lambda_weight, preferred_element_type=jnp.float32))

        def per_block(pieces):
            return block_terms(pieces[0], pieces[1], pieces[2], pieces[3], pieces[4], masks)
        near, state, total, cumulative, weights_all = lax.map(per_block, (query_rows.reshape(N_CTX, TOK_DEV, -1), key_rows.reshape(N_CTX, TOK_DEV, -1), value_rows.reshape(N_CTX, TOK_DEV, -1), lambdas.reshape(N_CTX, TOK_DEV, -1), decays.reshape(N_CTX, TOK_DEV, -1)))
        block_index = jnp.arange(N_CTX, dtype=jnp.int32)
        block_state = state
        block_total = total
        carry_decay = jnp.ones_like(total)
        query_blocks = query_rows.reshape(N_CTX, TOK_DEV, -1).astype(jnp.float32)
        mixed = near
        for level_bit in range(bits):
            partner = jnp.bitwise_xor(block_index, jnp.int32(1 << level_bit))
            other_state = block_state[partner]
            other_total = block_total[partner]
            upper = (block_index >> level_bit & 1).astype(jnp.float32)
            carried = (carry_decay[:, :, None, None] * other_state).astype(jnp.bfloat16)
            reach = jnp.einsum('jts,jhsd->jthd', query_blocks, carried.astype(jnp.float32), precision=HIGHEST)
            factor = weights_all[:, :, :, inner + level_bit] * jnp.exp(cumulative) * (scale * upper[:, None, None])
            mixed = mixed + factor[..., None] * reach
            if level_bit + 1 < bits:
                flag = upper[:, None, None, None] > 0
                block_state = jnp.where(flag, block_total[:, :, None, None] * other_state + block_state, other_total[:, :, None, None] * block_state + other_state)
                carry_decay = jnp.where(upper[:, None] > 0, other_total * carry_decay, carry_decay)
                block_total = block_total * other_total
        return finish(mixed, norm_gain).reshape(SEQUENCE_SPAN, -1)
    return lax.map(one_sequence, (inputs, log_decay))
```

```python
import functools
import math

import jax
import jax.numpy as jnp
from jax import lax
from jax.experimental import pallas as pl
from jax.experimental.pallas import tpu as pltpu
from jax.sharding import PartitionSpec as P

HIGHEST = lax.Precision.HIGHEST
F32 = jnp.float32
BF16 = jnp.bfloat16
BLOCK = 256
HALF = 128
LEVELS = 20
INNER = 9
BITS = 6
MASKS = (2, 6, 8, 24, 56)
HPC = 8
HPT = 6
VMEM_LIMIT = 56 * 1024 * 1024


def ring_x(step, n_dp, n_ctx):
    pairs = []
    for x in range(n_dp):
        for c in range(n_ctx):
            to = (x + (step if c % 2 == 0 else -step)) % n_dp
            pairs.append((x * n_ctx + c, to * n_ctx + c))
    return pairs


def ring_y(step, n_ctx):
    pairs = []
    for c in range(n_ctx):
        z, y, core = c >> 3, c >> 1 & 3, c & 1
        to = (y + (step if core == 0 else -step)) % 4
        pairs.append((c, z * 8 + to * 2 + core))
    return pairs


def xor_pairs(mask, n_ctx):
    return [(c, c ^ mask) for c in range(n_ctx)]


def whole(n):
    return [pl.BlockSpec(memory_space=pltpu.VMEM)] * n


def call(kernel, outs, args, smem=0, flops=0, nbytes=0, scratch=()):
    specs = [pl.BlockSpec(memory_space=pltpu.SMEM)] * smem + whole(len(args) - smem)
    return pl.pallas_call(
        kernel,
        out_shape=outs,
        in_specs=specs,
        out_specs=jax.tree.map(lambda _: pl.BlockSpec(memory_space=pltpu.VMEM), outs),
        scratch_shapes=list(scratch),
        compiler_params=pltpu.CompilerParams(vmem_limit_bytes=VMEM_LIMIT),
        cost_estimate=pl.CostEstimate(flops=flops, bytes_accessed=nbytes, transcendentals=0),
    )(*args)


def lam_slot(h):
    return h // HPT * HALF + h % HPT * LEVELS


def small_kernel(n, off_ref, tok_ref, gl_ref, *refs):
    pieces, (q_ref, k_ref, lam_ref) = refs[:n], refs[n:]
    total = None
    for p in range(n):
        depth = pieces[p].shape[0]
        columns = pl.ds(pl.multiple_of(off_ref[p], 256), depth)
        part = jnp.dot(tok_ref[:, columns], pieces[p][...], preferred_element_type=F32)
        total = part if total is None else total + part
    q_ref[...] = total[:, :HALF].astype(BF16)
    k_ref[...] = total[:, HALF : 2 * HALF].astype(BF16)
    lam = total[:, 2 * HALF :]
    soft = jnp.maximum(lam, 0.0) + jnp.log1p(jnp.exp(-jnp.abs(lam)))
    lam_ref[...] = soft * gl_ref[...]


def value_kernel(n, first, off_ref, tok_ref, *refs):
    base = None
    if not first:
        base, refs = refs[0], refs[1:]
    pieces, out_ref = refs[:n], refs[n]
    width = out_ref.shape[1]

    @pl.loop(0, width // 256)
    def _(j):
        cols = pl.ds(pl.multiple_of(j * 256, 256), 256)
        total = None if first else base[:, cols]
        for p in range(n):
            depth = pieces[p].shape[0]
            rows = pl.ds(pl.multiple_of(off_ref[p], 256), depth)
            part = jnp.dot(tok_ref[:, rows], pieces[p][:, cols], preferred_element_type=F32)
            total = part if total is None else total + part
        out_ref[:, cols] = total.astype(out_ref.dtype)


def state_kernel(k_ref, v_ref, remain_ref, tot_ref, chip_ref, low_ref):
    kt = jnp.transpose(k_ref[...].astype(F32))
    for h in range(HPC):
        cols = slice(h * HALF, (h + 1) * HALF)
        keyed = (kt * remain_ref[h : h + 1, :]).astype(BF16)
        low = jnp.dot(keyed[:, :BLOCK], v_ref[:BLOCK, cols], preferred_element_type=F32)
        high = jnp.dot(keyed[:, BLOCK:], v_ref[BLOCK:, cols], preferred_element_type=F32)
        low_ref[:, cols] = low.astype(BF16)
        chip_ref[:, cols] = tot_ref[h : h + 1, :] * low + high


def near_kernel(q_ref, k_ref, v_ref, lam_ref, cum_ref, cumt_ref, low_ref, out_ref):
    row = lax.broadcasted_iota(jnp.int32, (HALF, HALF), 0)
    col = lax.broadcasted_iota(jnp.int32, (HALF, HALF), 1)
    differ = jnp.bitwise_xor(row, col)
    level = jnp.zeros((HALF, HALF), jnp.int32)
    for power in range(7):
        level = level + jnp.where(differ >= 1 << power, 1, 0)
    causal = row >= col
    for b in range(2):
        r0 = b * BLOCK
        tiles = [slice(r0, r0 + HALF), slice(r0 + HALF, r0 + BLOCK)]
        scores = lax.dot_general(
            q_ref[r0 : r0 + BLOCK, :],
            k_ref[r0 : r0 + BLOCK, :],
            (((1,), (1,)), ((), ())),
            preferred_element_type=F32,
        )
        s00, s10, s11 = scores[:HALF, :HALF], scores[HALF:, :HALF], scores[HALF:, HALF:]
        for h in range(HPC):
            cols = slice(h * HALF, (h + 1) * HALF)
            slot = lam_slot(h)
            tile = slice(slot // HALF * HALF, slot // HALF * HALF + HALF)
            inner = slot % HALF
            lam0 = lam_ref[tiles[0], tile]
            lam1 = lam_ref[tiles[1], tile]
            index = level + inner
            w00 = jnp.take_along_axis(lam0, index, axis=1)
            w11 = jnp.take_along_axis(lam1, index, axis=1)
            w10 = jnp.broadcast_to(lam1[:, inner + 8 : inner + 9], (HALF, HALF))
            t0 = cum_ref[tiles[0], h : h + 1]
            t1 = cum_ref[tiles[1], h : h + 1]
            c0 = cumt_ref[h : h + 1, tiles[0]]
            c1 = cumt_ref[h : h + 1, tiles[1]]
            m00 = w00 * jnp.exp(jnp.where(causal, t0 - c0, -jnp.inf)) * s00
            m11 = w11 * jnp.exp(jnp.where(causal, t1 - c1, -jnp.inf)) * s11
            m10 = w10 * jnp.exp(t1 - c0) * s10
            v0 = v_ref[tiles[0], cols]
            v1 = v_ref[tiles[1], cols]
            out0 = jnp.dot(m00.astype(BF16), v0, preferred_element_type=F32)
            mix1 = jnp.concatenate([m10.astype(BF16), m11.astype(BF16)], axis=1)
            out1 = jnp.dot(mix1, v_ref[r0 : r0 + BLOCK, cols], preferred_element_type=F32)
            if b == 1:
                reach = jnp.dot(
                    q_ref[BLOCK:, :], low_ref[:, cols], preferred_element_type=F32
                )
                out0 = out0 + lam0[:, inner + INNER : inner + INNER + 1] * reach[:HALF]
                out1 = out1 + lam1[:, inner + INNER : inner + INNER + 1] * reach[HALF:]
            out_ref[tiles[0], cols] = out0
            out_ref[tiles[1], cols] = out1


def far_kernel(bits, last, q_ref, lam_ref, gain_ref, base_ref, *refs):
    carried, out_ref = refs[:-1], refs[-1]
    for h in range(HPC):
        cols = slice(h * HALF, (h + 1) * HALF)
        total = base_ref[:, cols]
        slot = lam_slot(h) + INNER
        for bit, ref in zip(bits, carried):
            reach = jnp.dot(q_ref[...], ref[:, cols], preferred_element_type=F32)
            total = total + lam_ref[:, slot + bit : slot + bit + 1] * reach
        if last:
            mean = jnp.mean(total * total, axis=1, keepdims=True)
            total = total * lax.rsqrt(mean + 1e-05) * gain_ref[:, cols]
        out_ref[:, cols] = total.astype(out_ref.dtype)


def per_device(inputs, query_weight, key_weight, value_weight, lambda_weight, log_decay, norm_gain):
    n_dp, n_ctx = lax.axis_size("dp"), lax.axis_size("ctx")
    x, ctx = lax.axis_index("dp"), lax.axis_index("ctx")
    core, y = ctx & 1, ctx >> 1 & 3
    sign = 1 - 2 * core
    rows = query_weight.shape[0]
    chunk = rows // 4
    half = value_weight.shape[1] // 2

    def px(a, step):
        return lax.ppermute(a, ("dp", "ctx"), ring_x(step, n_dp, n_ctx))

    def py(a, step):
        return lax.ppermute(a, "ctx", ring_y(step, n_ctx))

    def swap(a, mask):
        return lax.ppermute(a, "ctx", xor_pairs(mask, n_ctx))

    def in_order(mine, other, axis=0):
        low = jnp.where(core == 0, mine, other)
        high = jnp.where(core == 0, other, mine)
        return jnp.concatenate([low, high], axis=axis)

    mine = lax.dynamic_slice(value_weight, (y * chunk, core * half), (chunk, half))
    a1 = px(mine, 1)
    a2 = px(mine, -1)
    a3 = px(a1, 1)
    lam_half = lax.dynamic_slice(lambda_weight, (0, core * HPC * LEVELS), (rows, HPC * LEVELS))
    cut = HPT * LEVELS
    small = jnp.concatenate(
        [
            query_weight,
            key_weight,
            jnp.pad(lam_half[:, :cut], ((0, 0), (0, HALF - cut))),
            jnp.pad(lam_half[:, cut:], ((0, 0), (0, HALF - (HPC * LEVELS - cut)))),
        ],
        axis=1,
    )
    s1 = px(small, 1)
    s2 = px(small, -1)
    s3 = px(s1, 1)
    tokens = in_order(inputs[0], swap(inputs[0], 1))
    decay_mine = log_decay[0]
    decays = in_order(decay_mine, swap(decay_mine, 1))
    decays = lax.dynamic_slice(decays, (0, core * HPC), (2 * BLOCK, HPC))

    sources = [(a1, (x - sign) % n_dp), (a2, (x + sign) % n_dp), (a3, x ^ 2)]
    pieces, offsets = [], []
    early, early_at = [], []
    for piece, source in sources:
        b1 = py(piece, 1)
        b2 = py(piece, -1)
        b3 = py(b1, 1)
        early.append(piece)
        early_at.append(source * rows + y * chunk)
        pieces += [b1, b2, b3]
        offsets += [
            source * rows + (y - sign) % 4 * chunk,
            source * rows + (y + sign) % 4 * chunk,
            source * rows + (y ^ 2) * chunk,
        ]

    place = jnp.arange(BLOCK, dtype=jnp.int32)
    tri = (place[:, None] >= place[None, :]).astype(F32)
    pair = decays.reshape(2, BLOCK, HPC)
    cum = jnp.einsum("ts,bsh->bth", tri, pair, precision=HIGHEST)
    ends = cum[:, -1, :]
    scale = 1.0 / math.sqrt(HALF)
    total = ends[0] + ends[1]
    before = jnp.zeros_like(total)
    gains = [jnp.stack([jnp.zeros_like(cum[0]), scale * jnp.exp(cum[1])])]
    scale_other, scale_mine = [], []
    for bit, mask in zip(range(1, BITS), MASKS):
        upper = (ctx >> bit & 1) > 0
        lead = jnp.stack([before, before + ends[0]])
        gains.append(jnp.where(upper, scale * jnp.exp(cum + lead[:, None, :]), 0.0))
        other = swap(total, mask)
        scale_other.append(jnp.exp(jnp.where(upper, total, 0.0)))
        scale_mine.append(jnp.exp(jnp.where(upper, 0.0, other)))
        before = jnp.where(upper, before + other, before)
        total = total + other
    gl = jnp.concatenate(
        [
            jnp.full((2, BLOCK, HPC, INNER), scale, F32),
            jnp.stack(gains, axis=-1),
            jnp.zeros((2, BLOCK, HPC, LEVELS - INNER - BITS), F32),
        ],
        axis=-1,
    ).reshape(2 * BLOCK, HPC * LEVELS)
    gl = jnp.concatenate(
        [
            jnp.pad(gl[:, :cut], ((0, 0), (0, HALF - cut))),
            jnp.pad(gl[:, cut:], ((0, 0), (0, HALF - (HPC * LEVELS - cut)))),
        ],
        axis=1,
    )
    remain = jnp.exp(ends[:, None, :] - cum).reshape(2 * BLOCK, HPC).T
    high_total = jnp.broadcast_to(jnp.exp(ends[1])[:, None], (HPC, HALF))
    cum = cum.reshape(2 * BLOCK, HPC)
    cum_t = cum.T

    small_at = jnp.stack([x, (x - sign) % n_dp, (x + sign) % n_dp, x ^ 2]) * rows
    q, k, lam = call(
        functools.partial(small_kernel, 4),
        (
            jax.ShapeDtypeStruct((2 * BLOCK, HALF), BF16),
            jax.ShapeDtypeStruct((2 * BLOCK, HALF), BF16),
            jax.ShapeDtypeStruct((2 * BLOCK, 2 * HALF), F32),
        ),
        (small_at, tokens, gl, small, s1, s2, s3),
        smem=1,
        flops=2 * 512 * 4096 * 512,
        nbytes=8 << 20,
    )
    own = lax.dynamic_slice(value_weight, (0, core * half), (rows, half))
    first_at = jnp.stack([x * rows] + early_at)
    first = call(
        functools.partial(value_kernel, 4, True),
        jax.ShapeDtypeStruct((2 * BLOCK, half), F32),
        (first_at, tokens, own, *early),
        smem=1,
        flops=2 * 512 * 1792 * 1024,
        nbytes=8 << 20,
    )
    v = call(
        functools.partial(value_kernel, 9, False),
        jax.ShapeDtypeStruct((2 * BLOCK, half), BF16),
        (jnp.stack(offsets), tokens, first, *pieces),
        smem=1,
        flops=2 * 512 * 2304 * 1024,
        nbytes=12 << 20,
    )

    state, low_state = call(
        state_kernel,
        (
            jax.ShapeDtypeStruct((HALF, half), F32),
            jax.ShapeDtypeStruct((HALF, half), BF16),
        ),
        (k, v, remain, high_total),
        flops=2 * 512 * 128 * 1024,
        nbytes=2 << 20,
    )
    near = call(
        near_kernel,
        jax.ShapeDtypeStruct((2 * BLOCK, half), F32),
        (q, k, v, lam, cum, cum_t, low_state),
        flops=2 * 512 * 512 * 1024,
        nbytes=16 << 20,
    )
    carried = []
    for bit, mask in zip(range(1, BITS), MASKS):
        other = swap(state.astype(BF16), mask)
        carried.append(other)
        if bit + 1 < BITS:
            state = (
                jnp.repeat(scale_other[bit - 1], HALF)[None, :] * other.astype(F32)
                + jnp.repeat(scale_mine[bit - 1], HALF)[None, :] * state
            )
    gain = lax.dynamic_slice(norm_gain, (core * half,), (half,)).reshape(1, half)
    mixed = call(
        functools.partial(far_kernel, (1, 2, 3), False),
        jax.ShapeDtypeStruct((2 * BLOCK, half), F32),
        (q, lam, gain, near, *carried[:3]),
        flops=2 * 512 * 128 * 1024 * 3,
        nbytes=5 << 20,
    )
    out = call(
        functools.partial(far_kernel, (4, 5), True),
        jax.ShapeDtypeStruct((2 * BLOCK, half), BF16),
        (q, lam, gain, mixed, *carried[3:]),
        flops=2 * 512 * 128 * 1024 * 2,
        nbytes=4 << 20,
    )
    keep = lax.dynamic_slice(out, (core * BLOCK, 0), (BLOCK, half))
    give = lax.dynamic_slice(out, ((1 - core) * BLOCK, 0), (BLOCK, half))
    return in_order(keep, swap(give, 1), axis=1)[None]


def solution(mesh):
    return jax.shard_map(
        per_device,
        mesh=mesh,
        in_specs=(
            P("dp", "ctx", None),
            P("dp", None),
            P("dp", None),
            P("dp", None),
            P("dp", None),
            P("dp", "ctx", None),
            P(),
        ),
        out_specs=P("dp", "ctx", None),
        check_vma=False,
    )
```

```python
import functools
import math

import jax
import jax.numpy as jnp
from jax import lax
from jax.experimental import pallas as pl
from jax.experimental.pallas import tpu as pltpu
from jax.sharding import PartitionSpec as P

HIGHEST = lax.Precision.HIGHEST
F32 = jnp.float32
BF16 = jnp.bfloat16
BLOCK = 256
HALF = 128
LEVELS = 20
INNER = 9
BITS = 6
HPC = 4
MASKS = (6, 8, 24, 56)
BIG = 56
FINISH = BIG
EXTRA = 16


def ring_x(step, n_dp, n_ctx):
    pairs = []
    for x in range(n_dp):
        for c in range(n_ctx):
            to = (x + (step if c % 2 == 0 else -step)) % n_dp
            pairs.append((x * n_ctx + c, to * n_ctx + c))
    return pairs


def xor_pairs(mask, n_ctx):
    return [(c, c ^ mask) for c in range(n_ctx)]


def whole(n):
    return [pl.BlockSpec(memory_space=pltpu.VMEM)] * n


def call(kernel, outs, args, smem=0, flops=0, nbytes=0, mib=16):
    specs = [pl.BlockSpec(memory_space=pltpu.SMEM)] * smem + whole(len(args) - smem)
    return pl.pallas_call(
        kernel,
        out_shape=outs,
        in_specs=specs,
        out_specs=jax.tree.map(lambda _: pl.BlockSpec(memory_space=pltpu.VMEM), outs),
        compiler_params=pltpu.CompilerParams(vmem_limit_bytes=mib << 20),
        cost_estimate=pl.CostEstimate(flops=flops, bytes_accessed=nbytes, transcendentals=0),
    )(*args)


def exact(a, b, contract):
    return lax.dot_general(
        a, b, ((contract[:1], contract[1:]), ((), ())), precision=HIGHEST, preferred_element_type=F32
    )


def prep_kernel(at_ref, mine_ref, other_ref, cum_ref, cumt_ref, remain_ref, logs_ref, gl_ref):
    first = at_ref[0] == 0

    def ours_of(ref):
        rows = ref[:HPC, :]
        for i in range(1, 4):
            rows = jnp.where(at_ref[1] == i, ref[i * HPC : (i + 1) * HPC, :], rows)
        return rows

    mine, other = ours_of(mine_ref), ours_of(other_ref)
    row = lax.broadcasted_iota(jnp.int32, (BLOCK, BLOCK), 0)
    col = lax.broadcasted_iota(jnp.int32, (BLOCK, BLOCK), 1)
    tri = (row >= col).astype(F32)
    scale = 1.0 / math.sqrt(HALF)
    head = lax.broadcasted_iota(jnp.int32, (HPC, HALF), 0)
    lane = lax.broadcasted_iota(jnp.int32, (HPC, HALF), 1)
    local = lane * 3277 >> 16
    level = lane - local * LEVELS
    later_at = ((local == head) & (level > INNER) & (level < INNER + BITS)).astype(F32)
    first_at = ((local == head) & (level == INNER)).astype(F32)
    near_at = jnp.where(level[:1] < INNER, scale, 0.0)
    wide_row = lax.broadcasted_iota(jnp.int32, (HPC, HPC * HALF), 0)
    wide_col = lax.broadcasted_iota(jnp.int32, (HPC, HPC * HALF), 1)
    spread = (wide_col >> 7 == wide_row).astype(F32)
    lead = None
    for b in range(2):
        decay = jnp.where(first, mine, other) if b == 0 else jnp.where(first, other, mine)
        rows = slice(b * BLOCK, (b + 1) * BLOCK)
        across = exact(decay, tri, (1, 1))
        down = exact(tri, decay, (1, 1))
        cumt_ref[:, rows] = across
        remain_ref[:, rows] = jnp.exp(across[:, BLOCK - 1 :] - across)
        cum_ref[rows, :] = down
        end = down[BLOCK - 1 :, :]
        logs_ref[b : b + 1, :] = exact(jnp.broadcast_to(end, (HPC, HPC)), spread, (1, 0))[:1]
        growth = jnp.exp(down) * scale
        if b == 0:
            gl = exact(growth, later_at, (1, 0))
        else:
            later = jnp.exp(down + lead) * scale
            gl = exact(later, later_at, (1, 0)) + exact(growth, first_at, (1, 0))
        gl_ref[rows, :] = gl + near_at
        lead = end


def small_kernel(n, off_ref, mine_ref, other_ref, gl_ref, *refs):
    pieces, (row_ref, lam_ref) = refs[:n], refs[n:]
    for i, tok_ref in enumerate((mine_ref, other_ref)):
        rows = pl.ds(pl.multiple_of((off_ref[n] ^ i) * BLOCK, BLOCK), BLOCK)
        total = None
        for p in range(n):
            depth = pieces[p].shape[0]
            columns = pl.ds(pl.multiple_of(off_ref[p], BLOCK), depth)
            part = jnp.dot(tok_ref[:, columns], pieces[p][...], preferred_element_type=F32)
            total = part if total is None else total + part
        row_ref[rows, :] = total[:, :HALF].astype(BF16)
        lam = total[:, HALF:]
        soft = jnp.maximum(lam, 0.0) + jnp.log1p(jnp.exp(-jnp.abs(lam)))
        lam_ref[rows, :] = soft * gl_ref[rows, :]


def value_kernel(n, first, off_ref, mine_ref, other_ref, *refs):
    refs = list(refs)
    out_ref = refs.pop()
    base = None if first else refs.pop(0)
    for i, tok_ref in enumerate((mine_ref, other_ref)):
        rows = pl.ds(pl.multiple_of((off_ref[n] ^ i) * BLOCK, BLOCK), BLOCK)
        for start in range(0, out_ref.shape[1], BLOCK):
            cols = slice(start, start + BLOCK)
            total = None if first else base[rows, cols]
            for p in range(n):
                depth = refs[p].shape[0]
                columns = pl.ds(pl.multiple_of(off_ref[p], BLOCK), depth)
                part = jnp.dot(tok_ref[:, columns], refs[p][:, cols], preferred_element_type=F32)
                total = part if total is None else total + part
            out_ref[rows, cols] = total.astype(out_ref.dtype)


def put_payload(out_ref, state, log):
    out_ref[:HALF, :] = state.astype(BF16)
    rest = log
    parts = []
    for _ in range(3):
        part = rest.astype(BF16)
        rest = rest - part.astype(F32)
        parts.append(part.astype(F32))
    place = lax.broadcasted_iota(jnp.int32, (EXTRA, log.shape[1]), 0)
    tail = jnp.zeros((EXTRA, log.shape[1]), F32)
    for i, part in enumerate(parts):
        tail = jnp.where(place == i, part, tail)
    out_ref[HALF:, :] = tail.astype(BF16)


def take_payload(ref):
    tail = ref[HALF:, :].astype(F32)
    return ref[:HALF, :].astype(F32), tail[0:1, :] + tail[1:2, :] + tail[2:3, :]


def state_kernel(k_ref, v_ref, remain_ref, logs_ref, low_ref, send_ref):
    kt = jnp.transpose(k_ref[...].astype(F32))
    parts = []
    for h in range(HPC):
        cols = slice(h * HALF, (h + 1) * HALF)
        keyed = (kt * remain_ref[h : h + 1, :]).astype(BF16)
        low = jnp.dot(keyed[:, :BLOCK], v_ref[:BLOCK, cols], preferred_element_type=F32)
        high = jnp.dot(keyed[:, BLOCK:], v_ref[BLOCK:, cols], preferred_element_type=F32)
        low_ref[:, cols] = low.astype(BF16)
        parts.append(jnp.exp(logs_ref[1:2, cols]) * low + high)
    put_payload(send_ref, jnp.concatenate(parts, axis=1), logs_ref[0:1, :] + logs_ref[1:2, :])


def join_kernel(bit, at_ref, mine_ref, got_ref, out_ref):
    upper = (at_ref[0] >> bit & 1) > 0
    (s, log), (t, log_t) = take_payload(mine_ref), take_payload(got_ref)
    a = jnp.exp(jnp.where(upper, log, 0.0))
    b = jnp.exp(jnp.where(upper, 0.0, log_t))
    put_payload(out_ref, a * t + b * s, log + log_t)


def near_kernel(q_ref, k_ref, v_ref, lam_ref, cum_ref, cumt_ref, low_ref, out_ref):
    row = lax.broadcasted_iota(jnp.int32, (HALF, HALF), 0)
    col = lax.broadcasted_iota(jnp.int32, (HALF, HALF), 1)
    differ = jnp.bitwise_xor(row, col)
    level = jnp.zeros((HALF, HALF), jnp.int32)
    for power in range(7):
        level = level + jnp.where(differ >= 1 << power, 1, 0)
    causal = row >= col
    for b in range(2):
        r0 = b * BLOCK
        tiles = [slice(r0, r0 + HALF), slice(r0 + HALF, r0 + BLOCK)]
        scores = lax.dot_general(
            q_ref[r0 : r0 + BLOCK, :],
            k_ref[r0 : r0 + BLOCK, :],
            (((1,), (1,)), ((), ())),
            preferred_element_type=F32,
        )
        s00, s10, s11 = scores[:HALF, :HALF], scores[HALF:, :HALF], scores[HALF:, HALF:]
        for h in range(HPC):
            cols = slice(h * HALF, (h + 1) * HALF)
            inner = h * LEVELS
            lam0 = lam_ref[tiles[0], :]
            lam1 = lam_ref[tiles[1], :]
            index = level + inner
            w00 = jnp.take_along_axis(lam0, index, axis=1)
            w11 = jnp.take_along_axis(lam1, index, axis=1)
            w10 = jnp.broadcast_to(lam1[:, inner + 8 : inner + 9], (HALF, HALF))
            t0 = cum_ref[tiles[0], h : h + 1]
            t1 = cum_ref[tiles[1], h : h + 1]
            c0 = cumt_ref[h : h + 1, tiles[0]]
            c1 = cumt_ref[h : h + 1, tiles[1]]
            m00 = w00 * jnp.exp(jnp.where(causal, t0 - c0, -jnp.inf)) * s00
            m11 = w11 * jnp.exp(jnp.where(causal, t1 - c1, -jnp.inf)) * s11
            m10 = w10 * jnp.exp(t1 - c0) * s10
            v0 = v_ref[tiles[0], cols]
            out0 = jnp.dot(m00.astype(BF16), v0, preferred_element_type=F32)
            mix1 = jnp.concatenate([m10.astype(BF16), m11.astype(BF16)], axis=1)
            out1 = jnp.dot(mix1, v_ref[r0 : r0 + BLOCK, cols], preferred_element_type=F32)
            if b == 1:
                reach = jnp.dot(
                    q_ref[BLOCK:, :], low_ref[:, cols], preferred_element_type=F32
                )
                out0 = out0 + lam0[:, inner + INNER : inner + INNER + 1] * reach[:HALF]
                out1 = out1 + lam1[:, inner + INNER : inner + INNER + 1] * reach[HALF:]
            out_ref[tiles[0], cols] = out0
            out_ref[tiles[1], cols] = out1


def far_kernel(first, bits, outs, at_ref, q_ref, lam_ref, gain_ref, base_ref, *refs):
    n = len(refs) - outs
    got, out_refs = refs[:n], refs[n:]
    last = bits == BITS
    before = jnp.zeros((1, base_ref.shape[1]), F32)
    scales = []
    for i, ref in enumerate(got):
        upper = (at_ref[0] >> i & 1) > 0
        tail = ref[HALF:, :].astype(F32)
        scales.append(jnp.where(upper, jnp.exp(before), 0.0))
        before = before + jnp.where(upper, tail[0:1, :] + tail[1:2, :] + tail[2:3, :], 0.0)
    for pair in range(HPC // 2):
        both = slice(pair * BLOCK, (pair + 1) * BLOCK)
        carried = [
            (scales[bit - 1][:, both] * got[bit - 1][:HALF, both].astype(F32)).astype(BF16)
            for bit in range(first, bits)
        ]
        for o, out_ref in enumerate(out_refs):
            rows = pl.ds(pl.multiple_of(at_ref[1 + o], BLOCK), out_ref.shape[0])
            q, lam = q_ref[rows, :], lam_ref[rows, :]
            reach = [jnp.dot(q, c, preferred_element_type=F32) for c in carried]
            for i in range(2):
                cols = slice(pair * BLOCK + i * HALF, pair * BLOCK + (i + 1) * HALF)
                total = base_ref[rows, cols]
                for bit, part in zip(range(first, bits), reach):
                    slot = (2 * pair + i) * LEVELS + INNER + bit
                    total = total + lam[:, slot : slot + 1] * part[:, i * HALF : (i + 1) * HALF]
                if last:
                    mean = jnp.mean(total * total, axis=1, keepdims=True)
                    total = total * lax.rsqrt(mean + 1e-05) * gain_ref[:, cols]
                out_ref[:, cols] = total.astype(out_ref.dtype)


def place_kernel(at_ref, *refs):
    out_ref, width = refs[-1], refs[0].shape[1]
    for d, ref in enumerate(refs[:-1]):
        out_ref[:, pl.ds(pl.multiple_of((at_ref[0] ^ d) * width, width), width)] = ref[...]


def per_device(inputs, query_weight, key_weight, value_weight, lambda_weight, log_decay, norm_gain):
    n_dp, n_ctx = lax.axis_size("dp"), lax.axis_size("ctx")
    x, ctx = lax.axis_index("dp"), lax.axis_index("ctx")
    core, y0, y1 = ctx & 1, ctx >> 1 & 1, ctx >> 2 & 1
    sign = 1 - 2 * core
    quarter = core + 2 * (y0 ^ y1)
    rows = query_weight.shape[0]
    wide = value_weight.shape[1] // 4

    def px(a):
        return lax.ppermute(a, ("dp", "ctx"), ring_x(1, n_dp, n_ctx))

    def swap(a, mask):
        return lax.ppermute(a, "ctx", xor_pairs(mask, n_ctx))

    def after(a, *done):
        return lax.optimization_barrier((a, *done))[0]

    def shape(r, c, t):
        return jax.ShapeDtypeStruct((r, c), t)

    mine = inputs[0]
    decay_mine = log_decay[0].T
    decay_sib, decay_far, decay_farsib = [swap(decay_mine, m) for m in (1, 2, 3)]
    far = swap(after(mine, decay_far, decay_farsib), 2)
    weights_v = [lax.dynamic_slice(value_weight, (0, quarter * wide), (rows, wide))]
    weights_s = [
        jnp.concatenate(
            [
                jnp.where(core == 0, query_weight, key_weight),
                jnp.pad(
                    lax.dynamic_slice(lambda_weight, (0, quarter * HPC * LEVELS), (rows, HPC * LEVELS)),
                    ((0, 0), (0, HALF - HPC * LEVELS)),
                ),
            ],
            axis=1,
        )
    ]
    weights_s.append(px(weights_s[0]))
    weights_v.append(px(weights_v[0]))
    sib = swap(mine, 1)
    preps = []
    for pair in ((decay_mine, decay_sib), (decay_far, decay_farsib)):
        preps.append(
            call(
                prep_kernel,
                (
                    shape(2 * BLOCK, HPC, F32),
                    shape(HPC, 2 * BLOCK, F32),
                    shape(HPC, 2 * BLOCK, F32),
                    shape(2, wide, F32),
                    shape(2 * BLOCK, HALF, F32),
                ),
                (jnp.stack([core, quarter]), *pair),
                smem=1,
                flops=1 << 24,
                nbytes=1 << 20,
                mib=8,
            )
        )
    weights_s.append(px(weights_s[1]))
    weights_s.append(px(after(weights_s[2], preps[0][4], preps[1][4], sib)))
    weights_v.append(px(after(weights_v[1], weights_s[3])))
    weights_v.append(px(weights_v[2]))
    far = after(far, weights_v[2])
    far_sib = swap(far, 1)
    offsets = jnp.stack([(x - sign * i) % n_dp * rows for i in range(4)] + [core])

    chips = []
    for late in range(2):
        toks = (far, far_sib) if late else (mine, sib)
        cum, cum_t, remain, logs, gl = preps[late]
        made, lam = call(
            functools.partial(small_kernel, 4),
            (shape(2 * BLOCK, HALF, BF16), shape(2 * BLOCK, HALF, F32)),
            (offsets, *toks, gl, *weights_s),
            smem=1,
            flops=2 * 512 * 4096 * 256,
            nbytes=8 << 20,
        )
        fetched = swap(made, 1)
        q = jnp.where(core == 0, made, fetched)
        k = jnp.where(core == 0, fetched, made)
        part = call(
            functools.partial(value_kernel, 3, True),
            shape(2 * BLOCK, wide, F32),
            (jnp.concatenate([offsets[:3], offsets[4:]]), *toks, *weights_v[:3]),
            smem=1,
            flops=2 * 512 * 3072 * wide,
            nbytes=8 << 20,
        )
        chips.append([q, k, lam, part])

    last_v, *parts = lax.optimization_barrier((weights_v[3], chips[0][3], chips[1][3], chips[0][1], chips[1][1]))
    for late in range(2):
        toks = (far, far_sib) if late else (mine, sib)
        cum, cum_t, remain, logs, gl = preps[late]
        q, k, lam, _ = chips[late]
        k = parts[2 + late]
        v = call(
            functools.partial(value_kernel, 1, False),
            shape(2 * BLOCK, wide, BF16),
            (offsets[3:], *toks, parts[late], last_v),
            smem=1,
            flops=2 * 512 * 1024 * wide,
            nbytes=4 << 20,
        )
        payload = shape(HALF + EXTRA, wide, BF16)
        low_state, send = call(
            state_kernel,
            (shape(HALF, wide, BF16), payload),
            (k, v, remain, logs),
            flops=2 * 512 * 128 * wide,
            nbytes=1 << 20,
            mib=8,
        )
        near = call(
            near_kernel,
            shape(2 * BLOCK, wide, F32),
            (q, k, v, lam, cum, cum_t, low_state),
            flops=2 * 512 * 512 * wide,
            nbytes=8 << 20,
            mib=BIG,
        )
        chips[late] = [q, lam, near, send]

    at = ctx >> 1

    def join(bit, mine, got):
        return call(
            functools.partial(join_kernel, bit),
            payload,
            (at.reshape(1), mine, got),
            smem=1,
            flops=1 << 20,
            nbytes=1 << 20,
            mib=8,
        )

    send = join(0, chips[0][3], chips[1][3])
    got = []
    for i, mask in enumerate(MASKS):
        got.append(swap(send, mask))
        if i < 2:
            got[i], chips[1 - i][2] = lax.optimization_barrier((got[i], chips[1 - i][2]))
        if i + 1 < len(MASKS):
            send = join(i + 1, send, got[i])
    gain = lax.dynamic_slice(norm_gain, (quarter * wide,), (wide,)).reshape(1, wide)
    for late in range(2):
        q, lam, near, _ = chips[late]
        chips[late][2] = call(
            functools.partial(far_kernel, 1, 4, 1),
            shape(2 * BLOCK, wide, F32),
            (jnp.stack([at ^ late, 0 * at]), q, lam, gain, near, chips[1 - late][3], *got[:2]),
            smem=1,
            flops=2 * 512 * 128 * wide * 3,
            nbytes=4 << 20,
            mib=BIG,
        )
    got[3], chips[0][2], chips[1][2] = lax.optimization_barrier((got[3], chips[0][2], chips[1][2]))

    def finish(late):
        q, lam, mixed, _ = chips[late]
        return call(
            functools.partial(far_kernel, 4, BITS, 2),
            (shape(BLOCK, wide, BF16),) * 2,
            (
                jnp.stack([at ^ late, core * BLOCK, (1 - core) * BLOCK]),
                q, lam, gain, mixed, chips[1 - late][3], *got,
            ),
            smem=1,
            flops=2 * 512 * 128 * wide * 2,
            nbytes=4 << 20,
            mib=FINISH,
        )

    over, across = finish(1)
    over, across = swap(over, 2), swap(across, 3)
    keep, beside = finish(0)
    beside = swap(beside, 1)
    out = call(
        place_kernel,
        shape(BLOCK, 4 * wide, BF16),
        (quarter.reshape(1), keep, beside, over, across),
        smem=1,
        nbytes=2 << 20,
        mib=8,
    )
    return out[None]


def solution(mesh):
    return jax.shard_map(
        per_device,
        mesh=mesh,
        in_specs=(
            P("dp", "ctx", None),
            P("dp", None),
            P("dp", None),
            P("dp", None),
            P("dp", None),
            P("dp", "ctx", None),
            P(),
        ),
        out_specs=P("dp", "ctx", None),
        check_vma=False,
    )
```

```python
import functools
import math

import jax
import jax.numpy as jnp
from jax import lax
from jax.experimental import pallas as pl
from jax.experimental.pallas import tpu as pltpu
from jax.sharding import PartitionSpec as P

HIGHEST = lax.Precision.HIGHEST
F32 = jnp.float32
BF16 = jnp.bfloat16
BLOCK = 256
HALF = 128
LEVELS = 20
INNER = 9
BITS = 6
HPC = 4
MASKS = (6, 8, 24, 56)
BIG = 56
FINISH = BIG
EXTRA = 16


def ring_x(step, n_dp, n_ctx):
    pairs = []
    for x in range(n_dp):
        for c in range(n_ctx):
            to = (x + (step if c % 2 == 0 else -step)) % n_dp
            pairs.append((x * n_ctx + c, to * n_ctx + c))
    return pairs


def xor_pairs(mask, n_ctx):
    return [(c, c ^ mask) for c in range(n_ctx)]


def whole(n):
    return [pl.BlockSpec(memory_space=pltpu.VMEM)] * n


def call(kernel, outs, args, smem=0, flops=0, nbytes=0, mib=16):
    specs = [pl.BlockSpec(memory_space=pltpu.SMEM)] * smem + whole(len(args) - smem)
    return pl.pallas_call(
        kernel,
        out_shape=outs,
        in_specs=specs,
        out_specs=jax.tree.map(lambda _: pl.BlockSpec(memory_space=pltpu.VMEM), outs),
        compiler_params=pltpu.CompilerParams(vmem_limit_bytes=mib << 20),
        cost_estimate=pl.CostEstimate(flops=flops, bytes_accessed=nbytes, transcendentals=0),
    )(*args)


def exact(a, b, contract):
    return lax.dot_general(
        a, b, ((contract[:1], contract[1:]), ((), ())), precision=HIGHEST, preferred_element_type=F32
    )


def prep_kernel(at_ref, mine_ref, other_ref, cum_ref, cumt_ref, remain_ref, logs_ref, gl_ref):
    first = at_ref[0] == 0

    def ours_of(ref):
        rows = ref[:HPC, :]
        for i in range(1, 4):
            rows = jnp.where(at_ref[1] == i, ref[i * HPC : (i + 1) * HPC, :], rows)
        return rows

    mine, other = ours_of(mine_ref), ours_of(other_ref)
    row = lax.broadcasted_iota(jnp.int32, (BLOCK, BLOCK), 0)
    col = lax.broadcasted_iota(jnp.int32, (BLOCK, BLOCK), 1)
    tri = (row >= col).astype(F32)
    scale = 1.0 / math.sqrt(HALF)
    head = lax.broadcasted_iota(jnp.int32, (HPC, HALF), 0)
    lane = lax.broadcasted_iota(jnp.int32, (HPC, HALF), 1)
    local = lane * 3277 >> 16
    level = lane - local * LEVELS
    later_at = ((local == head) & (level > INNER) & (level < INNER + BITS)).astype(F32)
    first_at = ((local == head) & (level == INNER)).astype(F32)
    near_at = jnp.where(level[:1] < INNER, scale, 0.0)
    wide_row = lax.broadcasted_iota(jnp.int32, (HPC, HPC * HALF), 0)
    wide_col = lax.broadcasted_iota(jnp.int32, (HPC, HPC * HALF), 1)
    spread = (wide_col >> 7 == wide_row).astype(F32)
    lead = None
    for b in range(2):
        decay = jnp.where(first, mine, other) if b == 0 else jnp.where(first, other, mine)
        rows = slice(b * BLOCK, (b + 1) * BLOCK)
        across = exact(decay, tri, (1, 1))
        down = exact(tri, decay, (1, 1))
        cumt_ref[:, rows] = across
        remain_ref[:, rows] = jnp.exp(across[:, BLOCK - 1 :] - across)
        cum_ref[rows, :] = down
        end = down[BLOCK - 1 :, :]
        logs_ref[b : b + 1, :] = exact(jnp.broadcast_to(end, (HPC, HPC)), spread, (1, 0))[:1]
        growth = jnp.exp(down) * scale
        if b == 0:
            gl = exact(growth, later_at, (1, 0))
        else:
            later = jnp.exp(down + lead) * scale
            gl = exact(later, later_at, (1, 0)) + exact(growth, first_at, (1, 0))
        gl_ref[rows, :] = gl + near_at
        lead = end


def small_kernel(n, off_ref, mine_ref, other_ref, gl_ref, *refs):
    pieces, (row_ref, lam_ref) = refs[:n], refs[n:]
    for i, tok_ref in enumerate((mine_ref, other_ref)):
        rows = pl.ds(pl.multiple_of((off_ref[n] ^ i) * BLOCK, BLOCK), BLOCK)
        total = None
        for p in range(n):
            depth = pieces[p].shape[0]
            columns = pl.ds(pl.multiple_of(off_ref[p], BLOCK), depth)
            part = jnp.dot(tok_ref[:, columns], pieces[p][...], preferred_element_type=F32)
            total = part if total is None else total + part
        row_ref[rows, :] = total[:, :HALF].astype(BF16)
        lam = total[:, HALF:]
        soft = jnp.maximum(lam, 0.0) + jnp.log1p(jnp.exp(-jnp.abs(lam)))
        lam_ref[rows, :] = soft * gl_ref[rows, :]


def value_kernel(n, first, off_ref, mine_ref, other_ref, *refs):
    refs = list(refs)
    out_ref = refs.pop()
    base = None if first else refs.pop(0)
    for i, tok_ref in enumerate((mine_ref, other_ref)):
        rows = pl.ds(pl.multiple_of((off_ref[n] ^ i) * BLOCK, BLOCK), BLOCK)
        for start in range(0, out_ref.shape[1], BLOCK):
            cols = slice(start, start + BLOCK)
            total = None if first else base[rows, cols]
            for p in range(n):
                depth = refs[p].shape[0]
                columns = pl.ds(pl.multiple_of(off_ref[p], BLOCK), depth)
                part = jnp.dot(tok_ref[:, columns], refs[p][:, cols], preferred_element_type=F32)
                total = part if total is None else total + part
            out_ref[rows, cols] = total.astype(out_ref.dtype)


def put_payload(out_ref, state, log):
    out_ref[:HALF, :] = state.astype(BF16)
    rest = log
    parts = []
    for _ in range(3):
        part = rest.astype(BF16)
        rest = rest - part.astype(F32)
        parts.append(part.astype(F32))
    place = lax.broadcasted_iota(jnp.int32, (EXTRA, log.shape[1]), 0)
    tail = jnp.zeros((EXTRA, log.shape[1]), F32)
    for i, part in enumerate(parts):
        tail = jnp.where(place == i, part, tail)
    out_ref[HALF:, :] = tail.astype(BF16)


def take_payload(ref):
    tail = ref[HALF:, :].astype(F32)
    return ref[:HALF, :].astype(F32), tail[0:1, :] + tail[1:2, :] + tail[2:3, :]


def state_kernel(k_ref, v_ref, remain_ref, logs_ref, low_ref, send_ref):
    kt = jnp.transpose(k_ref[...].astype(F32))
    parts = []
    for h in range(HPC):
        cols = slice(h * HALF, (h + 1) * HALF)
        keyed = (kt * remain_ref[h : h + 1, :]).astype(BF16)
        low = jnp.dot(keyed[:, :BLOCK], v_ref[:BLOCK, cols], preferred_element_type=F32)
        high = jnp.dot(keyed[:, BLOCK:], v_ref[BLOCK:, cols], preferred_element_type=F32)
        low_ref[:, cols] = low.astype(BF16)
        parts.append(jnp.exp(logs_ref[1:2, cols]) * low + high)
    put_payload(send_ref, jnp.concatenate(parts, axis=1), logs_ref[0:1, :] + logs_ref[1:2, :])


def join_kernel(bit, at_ref, mine_ref, got_ref, out_ref):
    upper = (at_ref[0] >> bit & 1) > 0
    (s, log), (t, log_t) = take_payload(mine_ref), take_payload(got_ref)
    a = jnp.exp(jnp.where(upper, log, 0.0))
    b = jnp.exp(jnp.where(upper, 0.0, log_t))
    put_payload(out_ref, a * t + b * s, log + log_t)


def near_kernel(q_ref, k_ref, v_ref, lam_ref, cum_ref, cumt_ref, low_ref, out_ref):
    row = lax.broadcasted_iota(jnp.int32, (HALF, HALF), 0)
    col = lax.broadcasted_iota(jnp.int32, (HALF, HALF), 1)
    differ = jnp.bitwise_xor(row, col)
    level = jnp.zeros((HALF, HALF), jnp.int32)
    for power in range(7):
        level = level + jnp.where(differ >= 1 << power, 1, 0)
    causal = row >= col
    for b in range(2):
        r0 = b * BLOCK
        tiles = [slice(r0, r0 + HALF), slice(r0 + HALF, r0 + BLOCK)]
        scores = lax.dot_general(
            q_ref[r0 : r0 + BLOCK, :],
            k_ref[r0 : r0 + BLOCK, :],
            (((1,), (1,)), ((), ())),
            preferred_element_type=F32,
        )
        s00, s10, s11 = scores[:HALF, :HALF], scores[HALF:, :HALF], scores[HALF:, HALF:]
        for h in range(HPC):
            cols = slice(h * HALF, (h + 1) * HALF)
            inner = h * LEVELS
            lam0 = lam_ref[tiles[0], :]
            lam1 = lam_ref[tiles[1], :]
            index = level + inner
            w00 = jnp.take_along_axis(lam0, index, axis=1)
            w11 = jnp.take_along_axis(lam1, index, axis=1)
            w10 = jnp.broadcast_to(lam1[:, inner + 8 : inner + 9], (HALF, HALF))
            t0 = cum_ref[tiles[0], h : h + 1]
            t1 = cum_ref[tiles[1], h : h + 1]
            c0 = cumt_ref[h : h + 1, tiles[0]]
            c1 = cumt_ref[h : h + 1, tiles[1]]
            m00 = w00 * jnp.exp(jnp.where(causal, t0 - c0, -jnp.inf)) * s00
            m11 = w11 * jnp.exp(jnp.where(causal, t1 - c1, -jnp.inf)) * s11
            m10 = w10 * jnp.exp(t1 - c0) * s10
            v0 = v_ref[tiles[0], cols]
            out0 = jnp.dot(m00.astype(BF16), v0, preferred_element_type=F32)
            mix1 = jnp.concatenate([m10.astype(BF16), m11.astype(BF16)], axis=1)
            out1 = jnp.dot(mix1, v_ref[r0 : r0 + BLOCK, cols], preferred_element_type=F32)
            if b == 1:
                reach = jnp.dot(
                    q_ref[BLOCK:, :], low_ref[:, cols], preferred_element_type=F32
                )
                out0 = out0 + lam0[:, inner + INNER : inner + INNER + 1] * reach[:HALF]
                out1 = out1 + lam1[:, inner + INNER : inner + INNER + 1] * reach[HALF:]
            out_ref[tiles[0], cols] = out0
            out_ref[tiles[1], cols] = out1


def far_kernel(first, bits, outs, at_ref, q_ref, lam_ref, gain_ref, base_ref, *refs):
    n = len(refs) - outs
    got, out_refs = refs[:n], refs[n:]
    last = bits == BITS
    before = jnp.zeros((1, base_ref.shape[1]), F32)
    scales = []
    for i, ref in enumerate(got):
        upper = (at_ref[0] >> i & 1) > 0
        tail = ref[HALF:, :].astype(F32)
        scales.append(jnp.where(upper, jnp.exp(before), 0.0))
        before = before + jnp.where(upper, tail[0:1, :] + tail[1:2, :] + tail[2:3, :], 0.0)
    for pair in range(HPC // 2):
        both = slice(pair * BLOCK, (pair + 1) * BLOCK)
        carried = [
            (scales[bit - 1][:, both] * got[bit - 1][:HALF, both].astype(F32)).astype(BF16)
            for bit in range(first, bits)
        ]
        for o, out_ref in enumerate(out_refs):
            rows = pl.ds(pl.multiple_of(at_ref[1 + o], BLOCK), out_ref.shape[0])
            q, lam = q_ref[rows, :], lam_ref[rows, :]
            reach = [jnp.dot(q, c, preferred_element_type=F32) for c in carried]
            for i in range(2):
                cols = slice(pair * BLOCK + i * HALF, pair * BLOCK + (i + 1) * HALF)
                total = base_ref[rows, cols]
                for bit, part in zip(range(first, bits), reach):
                    slot = (2 * pair + i) * LEVELS + INNER + bit
                    total = total + lam[:, slot : slot + 1] * part[:, i * HALF : (i + 1) * HALF]
                if last:
                    mean = jnp.mean(total * total, axis=1, keepdims=True)
                    total = total * lax.rsqrt(mean + 1e-05) * gain_ref[:, cols]
                out_ref[:, cols] = total.astype(out_ref.dtype)


def place_kernel(at_ref, *refs):
    out_ref, width = refs[-1], refs[0].shape[1]
    for d, ref in enumerate(refs[:-1]):
        out_ref[:, pl.ds(pl.multiple_of((at_ref[0] ^ d) * width, width), width)] = ref[...]


def per_device(inputs, query_weight, key_weight, value_weight, lambda_weight, log_decay, norm_gain):
    n_dp, n_ctx = lax.axis_size("dp"), lax.axis_size("ctx")
    x, ctx = lax.axis_index("dp"), lax.axis_index("ctx")
    core, y0, y1 = ctx & 1, ctx >> 1 & 1, ctx >> 2 & 1
    sign = 1 - 2 * core
    quarter = core + 2 * (y0 ^ y1)
    rows = query_weight.shape[0]
    wide = value_weight.shape[1] // 4

    def px(a):
        return lax.ppermute(a, ("dp", "ctx"), ring_x(1, n_dp, n_ctx))

    def swap(a, mask):
        return lax.ppermute(a, "ctx", xor_pairs(mask, n_ctx))

    def after(a, *done):
        return lax.optimization_barrier((a, *done))[0]

    def shape(r, c, t):
        return jax.ShapeDtypeStruct((r, c), t)

    mine = inputs[0]
    decay_mine = log_decay[0].T
    weights_v = [lax.dynamic_slice(value_weight, (0, quarter * wide), (rows, wide))]
    weights_s = [
        jnp.concatenate(
            [
                jnp.where(core == 0, query_weight, key_weight),
                jnp.pad(
                    lax.dynamic_slice(lambda_weight, (0, quarter * HPC * LEVELS), (rows, HPC * LEVELS)),
                    ((0, 0), (0, HALF - HPC * LEVELS)),
                ),
            ],
            axis=1,
        )
    ]
    offsets = jnp.stack([(x - sign * i) % n_dp * rows for i in range(4)] + [core])
    cut = BLOCK // 2
    far_a = swap(mine[:cut], 2)
    weights_v.append(px(weights_v[0]))
    weights_s.append(px(weights_s[0]))
    decay_sib = swap(decay_mine, 1)
    sib = swap(mine, 1)
    weights_v[1], weights_s[1], far_a, sib, decay_sib, rest, decays = lax.optimization_barrier(
        (weights_v[1], weights_s[1], far_a, sib, decay_sib, mine[cut:], decay_mine)
    )
    far_b = swap(rest, 2)
    weights_v.append(px(weights_v[1]))
    weights_s.append(px(weights_s[1]))
    decay_far = swap(jnp.concatenate([decays, decay_sib], axis=0), 2)
    far_a_sib = swap(far_a, 1)

    def prep(pair):
        return call(
            prep_kernel,
            (
                shape(2 * BLOCK, HPC, F32),
                shape(HPC, 2 * BLOCK, F32),
                shape(HPC, 2 * BLOCK, F32),
                shape(2, wide, F32),
                shape(2 * BLOCK, HALF, F32),
            ),
            (jnp.stack([core, quarter]), *pair),
            smem=1,
            flops=1 << 24,
            nbytes=1 << 20,
            mib=8,
        )

    preps = [prep((decays, decay_sib))]

    def value(first, last, toks, base, kind):
        return call(
            functools.partial(value_kernel, last - first, base is None),
            shape(2 * BLOCK, wide, kind),
            (
                jnp.concatenate([offsets[first:last], offsets[4:]]),
                *toks,
                *([] if base is None else [base]),
                *weights_v[first:last],
            ),
            smem=1,
            flops=2 * 512 * 1024 * (last - first) * wide,
            nbytes=(4 + last - first) << 20,
        )

    parts = [value(0, 2, (mine, sib), None, F32)]
    weights_v[2], weights_s[2], far_b, far_a_sib, decay_far, parts[0] = lax.optimization_barrier(
        (weights_v[2], weights_s[2], far_b, far_a_sib, decay_far, parts[0])
    )
    far_b_sib = swap(far_b, 1)
    weights_v.append(px(weights_v[2]))
    weights_s.append(px(weights_s[2]))
    preps.append(prep((decay_far[:16], decay_far[16:])))
    far = jnp.concatenate([far_a, far_b], axis=0)
    far_sib = jnp.concatenate([far_a_sib, far_b_sib], axis=0)

    chips = []
    for late in range(2):
        toks = (far, far_sib) if late else (mine, sib)
        cum, cum_t, remain, logs, gl = preps[late]
        made, lam = call(
            functools.partial(small_kernel, 4),
            (shape(2 * BLOCK, HALF, BF16), shape(2 * BLOCK, HALF, F32)),
            (offsets, *toks, gl, *weights_s),
            smem=1,
            flops=2 * 512 * 4096 * 256,
            nbytes=8 << 20,
        )
        fetched = swap(made, 1)
        q = jnp.where(core == 0, made, fetched)
        k = jnp.where(core == 0, fetched, made)
        if late:
            parts.append(value(0, 3, toks, None, F32))
        chips.append([q, k, lam])

    weights_v[3], parts[1], chips[0][1], chips[1][1] = lax.optimization_barrier(
        (weights_v[3], parts[1], chips[0][1], chips[1][1])
    )
    for late in range(2):
        toks = (far, far_sib) if late else (mine, sib)
        cum, cum_t, remain, logs, gl = preps[late]
        q, k, lam = chips[late]
        v = value(2 + late, 4, toks, parts[late], BF16)
        payload = shape(HALF + EXTRA, wide, BF16)
        low_state, send = call(
            state_kernel,
            (shape(HALF, wide, BF16), payload),
            (k, v, remain, logs),
            flops=2 * 512 * 128 * wide,
            nbytes=1 << 20,
            mib=8,
        )
        near = call(
            near_kernel,
            shape(2 * BLOCK, wide, F32),
            (q, k, v, lam, cum, cum_t, low_state),
            flops=2 * 512 * 512 * wide,
            nbytes=8 << 20,
            mib=BIG,
        )
        chips[late] = [q, lam, near, send]

    at = ctx >> 1

    def join(bit, mine, got):
        return call(
            functools.partial(join_kernel, bit),
            payload,
            (at.reshape(1), mine, got),
            smem=1,
            flops=1 << 20,
            nbytes=1 << 20,
            mib=8,
        )

    send = join(0, chips[0][3], chips[1][3])
    got = []
    for i, mask in enumerate(MASKS):
        got.append(swap(send, mask))
        if i < 2:
            got[i], chips[1 - i][2] = lax.optimization_barrier((got[i], chips[1 - i][2]))
        if i + 1 < len(MASKS):
            send = join(i + 1, send, got[i])
    gain = lax.dynamic_slice(norm_gain, (quarter * wide,), (wide,)).reshape(1, wide)
    for late in range(2):
        q, lam, near, _ = chips[late]
        chips[late][2] = call(
            functools.partial(far_kernel, 1, 4, 1),
            shape(2 * BLOCK, wide, F32),
            (jnp.stack([at ^ late, 0 * at]), q, lam, gain, near, chips[1 - late][3], *got[:2]),
            smem=1,
            flops=2 * 512 * 128 * wide * 3,
            nbytes=4 << 20,
            mib=BIG,
        )
    got[3], chips[0][2], chips[1][2] = lax.optimization_barrier((got[3], chips[0][2], chips[1][2]))

    def finish(late):
        q, lam, mixed, _ = chips[late]
        return call(
            functools.partial(far_kernel, 4, BITS, 2),
            (shape(BLOCK, wide, BF16),) * 2,
            (
                jnp.stack([at ^ late, core * BLOCK, (1 - core) * BLOCK]),
                q, lam, gain, mixed, chips[1 - late][3], *got,
            ),
            smem=1,
            flops=2 * 512 * 128 * wide * 2,
            nbytes=4 << 20,
            mib=FINISH,
        )

    over, across = finish(1)
    over, across = swap(over, 2), swap(across, 3)
    keep, beside = finish(0)
    beside = swap(beside, 1)
    out = call(
        place_kernel,
        shape(BLOCK, 4 * wide, BF16),
        (quarter.reshape(1), keep, beside, over, across),
        smem=1,
        nbytes=2 << 20,
        mib=8,
    )
    return out[None]


def solution(mesh):
    return jax.shard_map(
        per_device,
        mesh=mesh,
        in_specs=(
            P("dp", "ctx", None),
            P("dp", None),
            P("dp", None),
            P("dp", None),
            P("dp", None),
            P("dp", "ctx", None),
            P(),
        ),
        out_specs=P("dp", "ctx", None),
        check_vma=False,
    )
```

```python
import functools
import math

import jax
import jax.numpy as jnp
from jax import lax
from jax.experimental import pallas as pl
from jax.experimental.pallas import tpu as pltpu
from jax.sharding import PartitionSpec as P

HIGHEST = lax.Precision.HIGHEST
F32 = jnp.float32
BF16 = jnp.bfloat16
BLOCK = 256
HALF = 128
LEVELS = 20
INNER = 9
BITS = 6
HPC = 4
MASKS = (6, 8, 24, 56)
BIG = 56
FINISH = 16
EXTRA = 16


def ring_x(step, n_dp, n_ctx):
    pairs = []
    for x in range(n_dp):
        for c in range(n_ctx):
            to = (x + (step if c % 2 == 0 else -step)) % n_dp
            pairs.append((x * n_ctx + c, to * n_ctx + c))
    return pairs


def xor_pairs(mask, n_ctx):
    return [(c, c ^ mask) for c in range(n_ctx)]


def whole(n):
    return [pl.BlockSpec(memory_space=pltpu.VMEM)] * n


def call(kernel, outs, args, smem=0, flops=0, nbytes=0, mib=16):
    specs = [pl.BlockSpec(memory_space=pltpu.SMEM)] * smem + whole(len(args) - smem)
    return pl.pallas_call(
        kernel,
        out_shape=outs,
        in_specs=specs,
        out_specs=jax.tree.map(lambda _: pl.BlockSpec(memory_space=pltpu.VMEM), outs),
        compiler_params=pltpu.CompilerParams(vmem_limit_bytes=mib << 20),
        cost_estimate=pl.CostEstimate(flops=flops, bytes_accessed=nbytes, transcendentals=0),
    )(*args)


def exact(a, b, contract):
    return lax.dot_general(
        a, b, ((contract[:1], contract[1:]), ((), ())), precision=HIGHEST, preferred_element_type=F32
    )


def prep_kernel(at_ref, mine_ref, other_ref, cum_ref, cumt_ref, remain_ref, logs_ref, gl_ref):
    first = at_ref[0] == 0

    def ours_of(ref):
        rows = ref[:HPC, :]
        for i in range(1, 4):
            rows = jnp.where(at_ref[1] == i, ref[i * HPC : (i + 1) * HPC, :], rows)
        return rows

    mine, other = ours_of(mine_ref), ours_of(other_ref)
    row = lax.broadcasted_iota(jnp.int32, (BLOCK, BLOCK), 0)
    col = lax.broadcasted_iota(jnp.int32, (BLOCK, BLOCK), 1)
    tri = (row >= col).astype(F32)
    scale = 1.0 / math.sqrt(HALF)
    head = lax.broadcasted_iota(jnp.int32, (HPC, HALF), 0)
    lane = lax.broadcasted_iota(jnp.int32, (HPC, HALF), 1)
    local = lane * 3277 >> 16
    level = lane - local * LEVELS
    later_at = ((local == head) & (level > INNER) & (level < INNER + BITS)).astype(F32)
    first_at = ((local == head) & (level == INNER)).astype(F32)
    near_at = jnp.where(level[:1] < INNER, scale, 0.0)
    wide_row = lax.broadcasted_iota(jnp.int32, (HPC, HPC * HALF), 0)
    wide_col = lax.broadcasted_iota(jnp.int32, (HPC, HPC * HALF), 1)
    spread = (wide_col >> 7 == wide_row).astype(F32)
    lead = None
    for b in range(2):
        decay = jnp.where(first, mine, other) if b == 0 else jnp.where(first, other, mine)
        rows = slice(b * BLOCK, (b + 1) * BLOCK)
        across = exact(decay, tri, (1, 1))
        down = exact(tri, decay, (1, 1))
        cumt_ref[:, rows] = across
        remain_ref[:, rows] = jnp.exp(across[:, BLOCK - 1 :] - across)
        cum_ref[rows, :] = down
        end = down[BLOCK - 1 :, :]
        logs_ref[b : b + 1, :] = exact(jnp.broadcast_to(end, (HPC, HPC)), spread, (1, 0))[:1]
        growth = jnp.exp(down) * scale
        if b == 0:
            gl = exact(growth, later_at, (1, 0))
        else:
            later = jnp.exp(down + lead) * scale
            gl = exact(later, later_at, (1, 0)) + exact(growth, first_at, (1, 0))
        gl_ref[rows, :] = gl + near_at
        lead = end


def small_kernel(n, off_ref, mine_ref, other_ref, gl_ref, *refs):
    pieces, (row_ref, lam_ref) = refs[:n], refs[n:]
    for i, tok_ref in enumerate((mine_ref, other_ref)):
        rows = pl.ds(pl.multiple_of((off_ref[n] ^ i) * BLOCK, BLOCK), BLOCK)
        total = None
        for p in range(n):
            depth = pieces[p].shape[0]
            columns = pl.ds(pl.multiple_of(off_ref[p], BLOCK), depth)
            part = jnp.dot(tok_ref[:, columns], pieces[p][...], preferred_element_type=F32)
            total = part if total is None else total + part
        row_ref[rows, :] = total[:, :HALF].astype(BF16)
        lam = total[:, HALF:]
        soft = jnp.maximum(lam, 0.0) + jnp.log1p(jnp.exp(-jnp.abs(lam)))
        lam_ref[rows, :] = soft * gl_ref[rows, :]


def value_kernel(n, first, off_ref, mine_ref, other_ref, *refs):
    refs = list(refs)
    out_ref = refs.pop()
    base = None if first else refs.pop(0)
    for i, tok_ref in enumerate((mine_ref, other_ref)):
        rows = pl.ds(pl.multiple_of((off_ref[n] ^ i) * BLOCK, BLOCK), BLOCK)
        for start in range(0, out_ref.shape[1], BLOCK):
            cols = slice(start, start + BLOCK)
            total = None if first else base[rows, cols]
            for p in range(n):
                depth = refs[p].shape[0]
                columns = pl.ds(pl.multiple_of(off_ref[p], BLOCK), depth)
                part = jnp.dot(tok_ref[:, columns], refs[p][:, cols], preferred_element_type=F32)
                total = part if total is None else total + part
            out_ref[rows, cols] = total.astype(out_ref.dtype)


def put_payload(out_ref, state, log):
    out_ref[:HALF, :] = state.astype(BF16)
    rest = log
    parts = []
    for _ in range(3):
        part = rest.astype(BF16)
        rest = rest - part.astype(F32)
        parts.append(part.astype(F32))
    place = lax.broadcasted_iota(jnp.int32, (EXTRA, log.shape[1]), 0)
    tail = jnp.zeros((EXTRA, log.shape[1]), F32)
    for i, part in enumerate(parts):
        tail = jnp.where(place == i, part, tail)
    out_ref[HALF:, :] = tail.astype(BF16)


def take_payload(ref):
    tail = ref[HALF:, :].astype(F32)
    return ref[:HALF, :].astype(F32), tail[0:1, :] + tail[1:2, :] + tail[2:3, :]


def state_kernel(k_ref, v_ref, remain_ref, logs_ref, low_ref, send_ref):
    kt = jnp.transpose(k_ref[...].astype(F32))
    parts = []
    for h in range(HPC):
        cols = slice(h * HALF, (h + 1) * HALF)
        keyed = (kt * remain_ref[h : h + 1, :]).astype(BF16)
        low = jnp.dot(keyed[:, :BLOCK], v_ref[:BLOCK, cols], preferred_element_type=F32)
        high = jnp.dot(keyed[:, BLOCK:], v_ref[BLOCK:, cols], preferred_element_type=F32)
        low_ref[:, cols] = low.astype(BF16)
        parts.append(jnp.exp(logs_ref[1:2, cols]) * low + high)
    put_payload(send_ref, jnp.concatenate(parts, axis=1), logs_ref[0:1, :] + logs_ref[1:2, :])


def join_kernel(bit, at_ref, mine_ref, got_ref, out_ref):
    upper = (at_ref[0] >> bit & 1) > 0
    (s, log), (t, log_t) = take_payload(mine_ref), take_payload(got_ref)
    a = jnp.exp(jnp.where(upper, log, 0.0))
    b = jnp.exp(jnp.where(upper, 0.0, log_t))
    put_payload(out_ref, a * t + b * s, log + log_t)


def near_kernel(q_ref, k_ref, v_ref, lam_ref, cum_ref, cumt_ref, low_ref, out_ref):
    row = lax.broadcasted_iota(jnp.int32, (HALF, HALF), 0)
    col = lax.broadcasted_iota(jnp.int32, (HALF, HALF), 1)
    differ = jnp.bitwise_xor(row, col)
    level = jnp.zeros((HALF, HALF), jnp.int32)
    for power in range(7):
        level = level + jnp.where(differ >= 1 << power, 1, 0)
    causal = row >= col
    for b in range(2):
        r0 = b * BLOCK
        tiles = [slice(r0, r0 + HALF), slice(r0 + HALF, r0 + BLOCK)]
        scores = lax.dot_general(
            q_ref[r0 : r0 + BLOCK, :],
            k_ref[r0 : r0 + BLOCK, :],
            (((1,), (1,)), ((), ())),
            preferred_element_type=F32,
        )
        s00, s10, s11 = scores[:HALF, :HALF], scores[HALF:, :HALF], scores[HALF:, HALF:]
        for h in range(HPC):
            cols = slice(h * HALF, (h + 1) * HALF)
            inner = h * LEVELS
            lam0 = lam_ref[tiles[0], :]
            lam1 = lam_ref[tiles[1], :]
            index = level + inner
            w00 = jnp.take_along_axis(lam0, index, axis=1)
            w11 = jnp.take_along_axis(lam1, index, axis=1)
            w10 = jnp.broadcast_to(lam1[:, inner + 8 : inner + 9], (HALF, HALF))
            t0 = cum_ref[tiles[0], h : h + 1]
            t1 = cum_ref[tiles[1], h : h + 1]
            c0 = cumt_ref[h : h + 1, tiles[0]]
            c1 = cumt_ref[h : h + 1, tiles[1]]
            m00 = w00 * jnp.exp(jnp.where(causal, t0 - c0, -jnp.inf)) * s00
            m11 = w11 * jnp.exp(jnp.where(causal, t1 - c1, -jnp.inf)) * s11
            m10 = w10 * jnp.exp(t1 - c0) * s10
            v0 = v_ref[tiles[0], cols]
            out0 = jnp.dot(m00.astype(BF16), v0, preferred_element_type=F32)
            mix1 = jnp.concatenate([m10.astype(BF16), m11.astype(BF16)], axis=1)
            out1 = jnp.dot(mix1, v_ref[r0 : r0 + BLOCK, cols], preferred_element_type=F32)
            if b == 1:
                reach = jnp.dot(
                    q_ref[BLOCK:, :], low_ref[:, cols], preferred_element_type=F32
                )
                out0 = out0 + lam0[:, inner + INNER : inner + INNER + 1] * reach[:HALF]
                out1 = out1 + lam1[:, inner + INNER : inner + INNER + 1] * reach[HALF:]
            out_ref[tiles[0], cols] = out0
            out_ref[tiles[1], cols] = out1


def far_kernel(first, bits, outs, at_ref, q_ref, lam_ref, gain_ref, base_ref, *refs):
    n = len(refs) - outs
    got, out_refs = refs[:n], refs[n:]
    last = bits == BITS
    before = jnp.zeros((1, base_ref.shape[1]), F32)
    scales = []
    for i, ref in enumerate(got):
        upper = (at_ref[0] >> i & 1) > 0
        tail = ref[HALF:, :].astype(F32)
        scales.append(jnp.where(upper, jnp.exp(before), 0.0))
        before = before + jnp.where(upper, tail[0:1, :] + tail[1:2, :] + tail[2:3, :], 0.0)
    for pair in range(HPC // 2):
        both = slice(pair * BLOCK, (pair + 1) * BLOCK)
        carried = [
            (scales[bit - 1][:, both] * got[bit - 1][:HALF, both].astype(F32)).astype(BF16)
            for bit in range(first, bits)
        ]
        for o, out_ref in enumerate(out_refs):
            rows = pl.ds(pl.multiple_of(at_ref[1 + o], BLOCK), out_ref.shape[0])
            q, lam = q_ref[rows, :], lam_ref[rows, :]
            reach = [jnp.dot(q, c, preferred_element_type=F32) for c in carried]
            for i in range(2):
                cols = slice(pair * BLOCK + i * HALF, pair * BLOCK + (i + 1) * HALF)
                total = base_ref[rows, cols]
                for bit, part in zip(range(first, bits), reach):
                    slot = (2 * pair + i) * LEVELS + INNER + bit
                    total = total + lam[:, slot : slot + 1] * part[:, i * HALF : (i + 1) * HALF]
                if last:
                    mean = jnp.mean(total * total, axis=1, keepdims=True)
                    total = total * lax.rsqrt(mean + 1e-05) * gain_ref[:, cols]
                out_ref[:, cols] = total.astype(out_ref.dtype)


def place_kernel(at_ref, *refs):
    out_ref, width = refs[-1], refs[0].shape[1]
    for d, ref in enumerate(refs[:-1]):
        out_ref[:, pl.ds(pl.multiple_of((at_ref[0] ^ d) * width, width), width)] = ref[...]


def per_device(inputs, query_weight, key_weight, value_weight, lambda_weight, log_decay, norm_gain):
    n_dp, n_ctx = lax.axis_size("dp"), lax.axis_size("ctx")
    x, ctx = lax.axis_index("dp"), lax.axis_index("ctx")
    core, y0, y1 = ctx & 1, ctx >> 1 & 1, ctx >> 2 & 1
    sign = 1 - 2 * core
    quarter = core + 2 * (y0 ^ y1)
    rows = query_weight.shape[0]
    wide = value_weight.shape[1] // 4

    def px(a):
        return lax.ppermute(a, ("dp", "ctx"), ring_x(1, n_dp, n_ctx))

    def swap(a, mask):
        return lax.ppermute(a, "ctx", xor_pairs(mask, n_ctx))

    def after(a, *done):
        return lax.optimization_barrier((a, *done))[0]

    def shape(r, c, t):
        return jax.ShapeDtypeStruct((r, c), t)

    mine = inputs[0]
    decay_mine = log_decay[0].T
    weights_v = [lax.dynamic_slice(value_weight, (0, quarter * wide), (rows, wide))]
    weights_s = [
        jnp.concatenate(
            [
                jnp.where(core == 0, query_weight, key_weight),
                jnp.pad(
                    lax.dynamic_slice(lambda_weight, (0, quarter * HPC * LEVELS), (rows, HPC * LEVELS)),
                    ((0, 0), (0, HALF - HPC * LEVELS)),
                ),
            ],
            axis=1,
        )
    ]
    offsets = jnp.stack([(x - sign * i) % n_dp * rows for i in range(4)] + [core])
    cut = BLOCK // 2
    far_a = swap(mine[:cut], 2)
    weights_v.append(px(weights_v[0]))
    weights_s.append(px(weights_s[0]))
    decay_sib = swap(decay_mine, 1)
    sib = swap(mine, 1)
    weights_v[1], weights_s[1], far_a, sib, decay_sib, rest, decays = lax.optimization_barrier(
        (weights_v[1], weights_s[1], far_a, sib, decay_sib, mine[cut:], decay_mine)
    )
    far_b = swap(rest, 2)
    weights_v.append(px(weights_v[1]))
    weights_s.append(px(weights_s[1]))
    decay_far = swap(jnp.concatenate([decays, decay_sib], axis=0), 2)
    far_a_sib = swap(far_a, 1)

    def prep(pair):
        return call(
            prep_kernel,
            (
                shape(2 * BLOCK, HPC, F32),
                shape(HPC, 2 * BLOCK, F32),
                shape(HPC, 2 * BLOCK, F32),
                shape(2, wide, F32),
                shape(2 * BLOCK, HALF, F32),
            ),
            (jnp.stack([core, quarter]), *pair),
            smem=1,
            flops=1 << 24,
            nbytes=1 << 20,
            mib=8,
        )

    preps = [prep((decays, decay_sib))]

    def value(first, last, toks, base, kind):
        return call(
            functools.partial(value_kernel, last - first, base is None),
            shape(2 * BLOCK, wide, kind),
            (
                jnp.concatenate([offsets[first:last], offsets[4:]]),
                *toks,
                *([] if base is None else [base]),
                *weights_v[first:last],
            ),
            smem=1,
            flops=2 * 512 * 1024 * (last - first) * wide,
            nbytes=(4 + last - first) << 20,
        )

    parts = [value(0, 2, (mine, sib), None, F32)]
    weights_v[2], weights_s[2], far_b, far_a_sib, decay_far, parts[0] = lax.optimization_barrier(
        (weights_v[2], weights_s[2], far_b, far_a_sib, decay_far, parts[0])
    )
    far_b_sib = swap(far_b, 1)
    weights_v.append(px(weights_v[2]))
    weights_s.append(px(weights_s[2]))
    preps.append(prep((decay_far[:16], decay_far[16:])))
    far = jnp.concatenate([far_a, far_b], axis=0)
    far_sib = jnp.concatenate([far_a_sib, far_b_sib], axis=0)

    chips = []
    for late in range(2):
        toks = (far, far_sib) if late else (mine, sib)
        cum, cum_t, remain, logs, gl = preps[late]
        made, lam = call(
            functools.partial(small_kernel, 4),
            (shape(2 * BLOCK, HALF, BF16), shape(2 * BLOCK, HALF, F32)),
            (offsets, *toks, gl, *weights_s),
            smem=1,
            flops=2 * 512 * 4096 * 256,
            nbytes=8 << 20,
        )
        fetched = swap(made, 1)
        q = jnp.where(core == 0, made, fetched)
        k = jnp.where(core == 0, fetched, made)
        if late:
            parts.append(value(0, 3, toks, None, F32))
        chips.append([q, k, lam])

    weights_v[3], parts[1], chips[0][1], chips[1][1] = lax.optimization_barrier(
        (weights_v[3], parts[1], chips[0][1], chips[1][1])
    )
    for late in range(2):
        toks = (far, far_sib) if late else (mine, sib)
        cum, cum_t, remain, logs, gl = preps[late]
        q, k, lam = chips[late]
        v = value(2 + late, 4, toks, parts[late], BF16)
        payload = shape(HALF + EXTRA, wide, BF16)
        low_state, send = call(
            state_kernel,
            (shape(HALF, wide, BF16), payload),
            (k, v, remain, logs),
            flops=2 * 512 * 128 * wide,
            nbytes=1 << 20,
            mib=8,
        )
        near = call(
            near_kernel,
            shape(2 * BLOCK, wide, F32),
            (q, k, v, lam, cum, cum_t, low_state),
            flops=2 * 512 * 512 * wide,
            nbytes=8 << 20,
            mib=BIG,
        )
        chips[late] = [q, lam, near, send]

    at = ctx >> 1

    def join(bit, mine, got):
        return call(
            functools.partial(join_kernel, bit),
            payload,
            (at.reshape(1), mine, got),
            smem=1,
            flops=1 << 20,
            nbytes=1 << 20,
            mib=8,
        )

    send = join(0, chips[0][3], chips[1][3])
    got = []
    for i, mask in enumerate(MASKS):
        got.append(swap(send, mask))
        if i < 2:
            got[i], chips[1 - i][2] = lax.optimization_barrier((got[i], chips[1 - i][2]))
        if i + 1 < len(MASKS):
            send = join(i + 1, send, got[i])
    gain = lax.dynamic_slice(norm_gain, (quarter * wide,), (wide,)).reshape(1, wide)
    for late in range(2):
        q, lam, near, _ = chips[late]
        chips[late][2] = call(
            functools.partial(far_kernel, 1, 4, 1),
            shape(2 * BLOCK, wide, F32),
            (jnp.stack([at ^ late, 0 * at]), q, lam, gain, near, chips[1 - late][3], *got[:2]),
            smem=1,
            flops=2 * 512 * 128 * wide * 3,
            nbytes=4 << 20,
            mib=BIG,
        )
    got[3], chips[0][2], chips[1][2] = lax.optimization_barrier((got[3], chips[0][2], chips[1][2]))

    def finish(late):
        q, lam, mixed, _ = chips[late]
        return call(
            functools.partial(far_kernel, 4, BITS, 2),
            (shape(BLOCK, wide, BF16),) * 2,
            (
                jnp.stack([at ^ late, core * BLOCK, (1 - core) * BLOCK]),
                q, lam, gain, mixed, chips[1 - late][3], *got,
            ),
            smem=1,
            flops=2 * 512 * 128 * wide * 2,
            nbytes=4 << 20,
            mib=FINISH,
        )

    over, across = finish(1)
    over, across = swap(over, 2), swap(across, 3)
    keep, beside = finish(0)
    beside = swap(beside, 1)
    out = call(
        place_kernel,
        shape(BLOCK, 4 * wide, BF16),
        (quarter.reshape(1), keep, beside, over, across),
        smem=1,
        nbytes=2 << 20,
        mib=8,
    )
    return out[None]


def solution(mesh):
    return jax.shard_map(
        per_device,
        mesh=mesh,
        in_specs=(
            P("dp", "ctx", None),
            P("dp", None),
            P("dp", None),
            P("dp", None),
            P("dp", None),
            P("dp", "ctx", None),
            P(),
        ),
        out_specs=P("dp", "ctx", None),
        check_vma=False,
    )
```
